32 devices in a mesh: groups: 2 (over y), dom: 4 (over z), pole: 2 (over x), vec: 2 (over core).
Axes of the slice: x: 2, y: 2, z: 4, core: 2. Of those that a mesh axis runs over, the one named last changes fastest.
Arguments:
- right_side: bfloat16 [8192, 256], P(('groups', 'dom'), 'vec'), parts along dimension 0, may hold values from -8 to 8
- inverse: bfloat16 [2, 2, 8192, 1024], P('pole', None, ('groups', 'dom')), parts along dimension 2, may hold values from -2 to 2
- coupling: bfloat16 [8, 2, 256, 256], P(('groups', 'dom')), parts along dimension 0, may hold values from -1 to 1, as said below
- weights: float32 [2, 2], P('pole'), may hold values from -3 to 3
Outputs:
- basis: bfloat16 [8192, 256], P(('groups', 'dom'), 'vec'), parts along dimension 0
- factor: float32 [512, 256], P('groups'), parts along dimension 0
The draws below stay inside these ranges and needn't reach their ends.
There are 2 independent parts, one for each index of `groups`. The reference program is written for one: setup_inputs(seed, part) draws one part's arguments, and reference() takes and returns one part's arrays. A program takes and returns all parts, laid end to end along the dimension named above; an argument that names none is the same for every part. Nothing has to cross between parts.
Inputs may be any that keep to these rules, and one draw needn't show every extreme that they name: coupling[d, 0] is the transpose of coupling[d - 1, 1]; coupling[0, 0] and coupling[3, 1] are zero.
All inputs are finite; a program needn't handle non-finite values.
Results may differ from the reference program's by a relative error of at most 0.0052.
Values may be sent and summed in bfloat16 or wider, within the bound.
A program may use at most 64 MiB of HBM per device.

```python
import math
import jax
import jax.numpy as jnp
from jax import lax

B = 1024
E = 256
M = 256
SWEEPS = 2
DOMAINS = 4
ROWS = 4096
POLES = 2


def draw_right_side(key, part):
    key = jax.random.fold_in(key, 11)
    keys = jax.random.split(key, 4)
    base = jax.random.normal(keys[0], (ROWS, M), jnp.float32)
    scale = jnp.exp(jax.random.uniform(keys[1], (ROWS, 1), jnp.float32, math.log(0.3), math.log(3.0)))
    mix = 0.6
    shared = jax.random.normal(keys[2], (ROWS, 1), jnp.float32) * jax.random.normal(keys[3], (1, M), jnp.float32)
    return jnp.clip(scale * (base + mix * shared), -8.0, 8.0).astype(jnp.bfloat16)


def draw_inverse(key, part):
    key = jax.random.fold_in(key, 22)
    keys = jax.random.split(key, 3)
    shape = (POLES, 2, ROWS, B)
    spread = 0.6 / math.sqrt(B)
    off = jnp.clip(jax.random.normal(keys[0], shape, jnp.float32), -5.0, 5.0) * spread
    row = jax.lax.broadcasted_iota(jnp.int32, (ROWS, B), 0) % B
    col = jax.lax.broadcasted_iota(jnp.int32, (ROWS, B), 1)
    eye = (row == col).astype(jnp.float32)
    real_diag = jax.random.uniform(keys[1], (POLES, 1, ROWS, 1), jnp.float32, 0.5, 1.0)
    imag_diag = jax.random.uniform(keys[2], (POLES, 1, ROWS, 1), jnp.float32, -0.6, 0.6)
    diag = jnp.concatenate([real_diag, imag_diag], axis=1)
    return (off + eye * diag).astype(jnp.bfloat16)


def draw_coupling(key, part):
    key = jax.random.fold_in(key, 33)
    spread = 0.25 / math.sqrt(E)
    base = jnp.clip(jax.random.normal(key, (DOMAINS, E, E), jnp.float32), -5.0, 5.0) * spread
    index = jax.lax.broadcasted_iota(jnp.int32, (DOMAINS, 1, 1), 0)
    after = base * (index < DOMAINS - 1).astype(jnp.float32)
    shifted = jnp.concatenate([jnp.zeros((1, E, E), jnp.float32), jnp.swapaxes(after[:-1], 1, 2)], axis=0)
    return jnp.stack([shifted, after], axis=1).astype(jnp.bfloat16)


def block_levels(key, shape, pieces, smallest, top_value):
    def one(position, parts):
        heights = jax.random.uniform(jax.random.fold_in(jax.random.fold_in(key, 6), position), (parts,), jnp.float32, smallest / len(pieces), top_value / len(pieces))
        return jnp.repeat(jnp.exp(heights), shape[position] // parts).reshape((-1,) + (1,) * (len(shape) - position - 1))

    gain = one(*pieces[0])
    for cut in pieces[1:]:
        gain = gain * one(*cut)
    return gain


def bell_draw(own_key, shape, width, reach, pieces=(), held_as=jnp.bfloat16):
    values = jax.random.normal(own_key, shape, jnp.float32) * width
    if len(pieces) > 0:
        values = block_levels(own_key, shape, pieces, -0.22, 0.18) * values
    return jnp.clip(values, min=-reach, max=reach).astype(held_as)


def setup_inputs(seed: int = 0, part: int = 0) -> dict:
    seeds = jax.random.split(jax.random.key(seed), 5)
    part_splits = jax.random.split(jax.random.fold_in(seeds[4], part), 5)
    return {
        "right_side": draw_right_side(jax.random.fold_in(jax.random.fold_in(seeds[4], part), 71), part),
        "inverse": draw_inverse(jax.random.fold_in(jax.random.fold_in(seeds[4], part), 71), part),
        "coupling": draw_coupling(jax.random.fold_in(jax.random.fold_in(seeds[4], part), 71), part),
        "weights": bell_draw(seeds[3], (POLES, 2), 1.0, 3.0, ((0, 2),), jnp.float32),
    }


def apply_blocks(inv, real_part, imag_part):
    hi = lax.Precision.HIGHEST
    real = jnp.einsum('dij,djm->dim', inv[0], real_part, precision=hi) - jnp.einsum('dij,djm->dim', inv[1], imag_part, precision=hi)
    imag = jnp.einsum('dij,djm->dim', inv[0], imag_part, precision=hi) + jnp.einsum('dij,djm->dim', inv[1], real_part, precision=hi)
    return jnp.stack([real, imag])

def neighbours(field, coupling, source):
    hi = lax.Precision.HIGHEST
    couple = coupling.astype(jnp.float32)
    last = field[:, :, B - E:, :].astype(jnp.float32)
    first = field[:, :, :E, :].astype(jnp.float32)
    zero = jnp.zeros((2, 1, E, M), jnp.float32)
    before = jnp.concatenate([zero, last[:, :-1]], axis=1)
    after = jnp.concatenate([first[:, 1:], zero], axis=1)
    top = jnp.einsum('dab,cdbm->cdam', couple[:, 0], before, precision=hi)
    bottom = jnp.einsum('dab,cdbm->cdam', couple[:, 1], after, precision=hi)
    rhs = jnp.stack([source, jnp.zeros_like(source)])
    rhs = rhs.at[:, :, :E].add(top).at[:, :, B - E:].add(bottom)
    return lax.optimization_barrier(rhs.astype(jnp.bfloat16))

def reference(right_side, inverse, coupling, weights):
    source = right_side.astype(jnp.float32).reshape(DOMAINS, B, M)
    total = jnp.zeros((DOMAINS, B, M), jnp.float32)
    for pole in range(POLES):
        inv = inverse[pole].astype(jnp.float32).reshape(2, DOMAINS, B, B)
        field = apply_blocks(inv, source, jnp.zeros_like(source))
        field = lax.optimization_barrier(field.astype(jnp.bfloat16))
        for sweep in range(SWEEPS):
            rhs = neighbours(field, coupling, source).astype(jnp.float32)
            field = apply_blocks(inv, rhs[0], rhs[1])
            if sweep < SWEEPS - 1:
                field = lax.optimization_barrier(field.astype(jnp.bfloat16))
        total = total + weights[pole, 0] * field[0] - weights[pole, 1] * field[1]
    filtered = total.reshape(ROWS, M)
    gram = jnp.dot(filtered.T, filtered, precision=lax.Precision.HIGHEST) / ROWS
    factor = jnp.linalg.cholesky(gram)
    solved = lax.linalg.triangular_solve(factor, filtered, left_side=False, lower=True, transpose_a=True)
    return (solved.astype(jnp.bfloat16), factor)
```

```python
import functools

import jax
import jax.numpy as jnp
from jax import lax
from jax.experimental import pallas as pl
from jax.experimental.pallas import tpu as pltpu
from jax.sharding import PartitionSpec as P

MESH = pl.DeviceIdType.MESH
HI = lax.Precision.HIGHEST
F32 = jnp.float32
BF16 = jnp.bfloat16
CHUNKS = 4


def mm(a, b):
    return jnp.dot(a, b, preferred_element_type=F32)


def tmm(a, b):
    return lax.dot_general(
        a, b, (((0,), (0,)), ((), ())), precision=HI, preferred_element_type=F32
    )


def hmm(a, b):
    return jnp.dot(a, b, precision=HI, preferred_element_type=F32)


def filter_kernel(
    nd, np_, x_ref, inv_ref, k_ref, w_ref, q_ref, g_ref,
    y0, edges, ends, pbuf, dbuf, gpart, gslot,
    e_send, e_recv, p_send, p_recv, d_send, d_recv, v_send, v_recv,
    r_send, r_recv, a_send, a_recv, f_send, f_recv,
):
    d = lax.axis_index("dom")
    p = lax.axis_index("pole")
    v = lax.axis_index("vec")
    rows, width = x_ref.shape
    edge = k_ref.shape[2]
    tall = rows // CHUNKS
    piece = g_ref.shape[1] // nd
    a_ref, c_ref = inv_ref.at[0, 0], inv_ref.at[0, 1]
    has_low, has_high = d > 0, d < nd - 1

    def dom(k):
        return {"dom": lax.rem(d + k, nd)}

    def pole(k):
        return {"pole": lax.rem(p + k, np_)}

    other = {"vec": 1 - v}

    barrier = pltpu.get_barrier_semaphore()
    for k in range(1, nd):
        pl.semaphore_signal(barrier, inc=1, device_id=dom(k), device_id_type=MESH)
    for k in range(1, np_):
        pl.semaphore_signal(barrier, inc=1, device_id=pole(k), device_id_type=MESH)
    pl.semaphore_signal(barrier, inc=1, device_id=other, device_id_type=MESH)

    @pl.when(jnp.logical_not(has_low))
    def _():
        ends[0, 0] = jnp.zeros(ends.shape[2:], BF16)
        ends[1, 0] = jnp.zeros(ends.shape[2:], BF16)

    @pl.when(jnp.logical_not(has_high))
    def _():
        ends[0, 1] = jnp.zeros(ends.shape[2:], BF16)
        ends[1, 1] = jnp.zeros(ends.shape[2:], BF16)

    pl.semaphore_wait(barrier, nd + np_ - 1)

    def copy(src, dst, send, recv, device):
        return pltpu.make_async_remote_copy(
            src_ref=src, dst_ref=dst, send_sem=send, recv_sem=recv,
            device_id=device, device_id_type=MESH,
        )

    def swap_ends(s):
        up = copy(edges.at[s, 1], ends.at[s, 0], e_send.at[s, 0], e_recv.at[s, 0], {"dom": d + 1})
        down = copy(edges.at[s, 0], ends.at[s, 1], e_send.at[s, 1], e_recv.at[s, 1], {"dom": d - 1})
        return up, down

    def start_ends(s):
        up, down = swap_ends(s)
        pl.when(has_high)(up.start)
        pl.when(has_low)(down.start)

    def wait_ends(s):
        up, down = swap_ends(s)
        pl.when(has_low)(up.wait_recv)
        pl.when(has_high)(down.wait_recv)
        pl.when(has_high)(up.wait_send)
        pl.when(has_low)(down.wait_send)

    x = x_ref[...]

    def first(lo):
        y0[lo : lo + edge, :width] = mm(a_ref[lo : lo + edge, :], x)
        y0[lo : lo + edge, width:] = mm(c_ref[lo : lo + edge, :], x)

    last = rows - edge
    for n, lo in enumerate((0, last)):
        first(lo)
        edges[0, n] = y0[lo : lo + edge, :].astype(BF16)
    start_ends(0)

    for lo in range(edge, last, edge):
        first(lo)
    w0, w1 = w_ref[0, 0], w_ref[0, 1]

    def source_part(lo, count):
        return w0 * y0[lo : lo + count, :width] - w1 * y0[lo : lo + count, width:]

    for lo in range(0, rows, tall):
        pbuf[p, lo : lo + tall] = source_part(lo, tall).astype(BF16)
    p_copies = [
        copy(pbuf.at[p], pbuf.at[p], p_send.at[k], p_recv.at[k], pole(k)) for k in range(1, np_)
    ]
    for c in p_copies:
        c.start()

    wait_ends(0)

    def turned(u):
        return jnp.concatenate([-u[:, width:], u[:, :width]], axis=1)

    tops = [mm(k_ref[0, n], ends[0, n]) for n in range(2)]
    plain = [t.astype(BF16) for t in tops]
    swapped = [turned(t).astype(BF16) for t in tops]
    for n, lo in enumerate((0, last)):
        total = y0[lo : lo + edge, :]
        for m, col in enumerate((0, last)):
            total += mm(a_ref[lo : lo + edge, col : col + edge], plain[m])
            total += mm(c_ref[lo : lo + edge, col : col + edge], swapped[m])
        edges[1, n] = total.astype(BF16)
    start_ends(1)
    wait_ends(1)

    tops = [mm(k_ref[0, n], ends[1, n]) for n in range(2)]
    gs = [(w0 * t[:, :width] - w1 * t[:, width:]).astype(BF16) for t in tops]
    hs = [(-w0 * t[:, width:] - w1 * t[:, :width]).astype(BF16) for t in tops]
    d_copies = []
    for i in range(CHUNKS):
        lo = i * tall
        part = source_part(lo, tall)
        total = part - part.astype(BF16).astype(F32)
        for m, col in enumerate((0, last)):
            total += mm(a_ref[lo : lo + tall, col : col + edge], gs[m])
            total += mm(c_ref[lo : lo + tall, col : col + edge], hs[m])
        dbuf[p, lo : lo + tall] = total.astype(BF16)
        here = dbuf.at[p, lo : lo + tall]
        d_copies.append([
            copy(here, here, d_send.at[i, k], d_recv.at[i, k], pole(k)) for k in range(1, np_)
        ])
        for c in d_copies[-1]:
            c.start()

    for c in p_copies:
        c.wait()
    v_copies = []
    for i in range(CHUNKS):
        lo = i * tall
        for c in d_copies[i]:
            c.wait()
        total = jnp.zeros((tall, width), F32)
        for q in range(np_):
            total += pbuf[q, lo : lo + tall].astype(F32) + dbuf[q, lo : lo + tall].astype(F32)
        q_ref[v, lo : lo + tall] = total
        here = q_ref.at[v, lo : lo + tall]
        v_copies.append(copy(here, here, v_send.at[i], v_recv.at[i], other))
        v_copies[-1].start()

    sums = [jnp.zeros((width, width), F32) for _ in range(2)]
    for i in range(CHUNKS):
        lo = i * tall
        v_copies[i].wait()
        mine = q_ref[v, lo : lo + tall]
        for u in range(2):
            sums[u] += tmm(q_ref[u, lo : lo + tall], mine)
    for u in range(2):
        gpart[u * width : (u + 1) * width] = sums[u]

    def own(k):
        return pl.ds(pl.multiple_of(lax.rem(d + k, nd) * piece, piece), piece)

    r_copies = [
        copy(gpart.at[own(k)], gslot.at[d], r_send.at[k], r_recv.at[k], dom(k))
        for k in range(1, nd)
    ]
    for c in r_copies:
        c.start()
    gslot[d] = gpart[own(0)]
    for c in r_copies:
        c.wait()
    total = gslot[0]
    for q in range(1, nd):
        total += gslot[q]
    g_ref[v, own(0)] = total
    here = g_ref.at[v, own(0)]
    a_copies = [copy(here, here, a_send.at[k], a_recv.at[k], dom(k)) for k in range(1, nd)]
    for c in a_copies:
        c.start()
    f_copies = []
    for k in range(nd):
        if k > 0:
            a_copies[k - 1].wait_recv()
        here = g_ref.at[v, own(nd - k)]
        f_copies.append(copy(here, here, f_send.at[k], f_recv.at[k], other))
        f_copies[-1].start()
    for c in a_copies:
        c.wait_send()
    for c in f_copies:
        c.wait()


def eliminate(w):
    n = w.shape[0]
    sub = lax.broadcasted_iota(jnp.int32, (8, n), 0)
    lane = lax.broadcasted_iota(jnp.int32, (8, n), 1)
    groups = n // 8
    ws = [w[8 * g : 8 * g + 8] for g in range(groups)]
    es = [(lane == sub + 8 * g).astype(F32) for g in range(groups)]
    upper, lower = [], []
    for b in range(groups):
        k = 8 * b
        pw, pe = ws[b], es[b]
        cols = [jnp.broadcast_to(pw[:, k + j : k + j + 1], (8, n)) for j in range(8)]
        far = [
            [jnp.broadcast_to(ws[g][:, k + j : k + j + 1], (8, n)) for j in range(8)]
            for g in range(b + 1, groups)
        ]
        uw, ue = jnp.zeros_like(pw), jnp.zeros_like(pe)
        for j in range(8):
            at = sub == j
            c = cols[j]
            pivot = c[j : j + 1]
            root = lax.rsqrt(pivot)
            inverse = 1.0 / pivot
            rw, re = pw[j : j + 1], pe[j : j + 1]
            uw = jnp.where(at, rw * root, uw)
            ue = jnp.where(at, re * root, ue)
            rw, re = rw * inverse, re * inverse
            pw = jnp.where(at, rw, pw - c * rw)
            pe = jnp.where(at, re, pe - c * re)
            for m in range(j + 1, 8):
                rc = cols[m][j : j + 1] * inverse
                cols[m] = jnp.where(at, rc, cols[m] - c * rc)
        upper.append(uw)
        lower.append(ue)
        for g in range(b + 1, groups):
            for j in range(8):
                c = far[g - b - 1][j]
                ws[g] = ws[g] - c * pw[j : j + 1]
                es[g] = es[g] - c * pe[j : j + 1]
    u = jnp.concatenate(upper, axis=0)
    l = jnp.concatenate(lower, axis=0)
    row = lax.broadcasted_iota(jnp.int32, (n, n), 0)
    col = lax.broadcasted_iota(jnp.int32, (n, n), 1)
    return jnp.where(row <= col, u, 0.0), jnp.where(row >= col, l, 0.0)


def solve_kernel(rows_total, q_ref, g_ref, basis_ref, factor_ref):
    v = lax.axis_index("vec")
    width = g_ref.shape[2]
    scale = 1.0 / rows_total
    u11, i11 = eliminate(g_ref[0, :width] * scale)
    u12 = hmm(i11, g_ref[1, :width] * scale)
    schur = g_ref[1, width:] * scale - tmm(u12, u12)
    u22, i22 = eliminate(schur)
    factor_ref[:width, :width] = u11.T
    factor_ref[:width, width:] = jnp.zeros((width, width), F32)
    factor_ref[width:, :width] = u12.T
    factor_ref[width:, width:] = u22.T

    def times(a, b):
        return lax.dot_general(
            a, b, (((1,), (1,)), ((), ())), precision=HI, preferred_element_type=F32
        )

    @pl.when(v == 0)
    def _():
        basis_ref[...] = times(q_ref[0], i11).astype(BF16)

    @pl.when(v == 1)
    def _():
        i21 = -hmm(i22, tmm(u12, i11))
        basis_ref[...] = (times(q_ref[0], i21) + times(q_ref[1], i22)).astype(BF16)


def body(right_side, inverse, coupling, weights):
    rows, width = right_side.shape
    edge = coupling.shape[2]
    nd, np_ = lax.axis_size("dom"), lax.axis_size("pole")
    vmem = pl.BlockSpec(memory_space=pltpu.VMEM)
    smem = pl.BlockSpec(memory_space=pltpu.SMEM)
    dma = pltpu.SemaphoreType.DMA
    q, g = pl.pallas_call(
        functools.partial(filter_kernel, nd, np_),
        out_shape=(
            jax.ShapeDtypeStruct((2, rows, width), F32),
            jax.ShapeDtypeStruct((2, 2 * width, width), F32),
        ),
        in_specs=[vmem, vmem, vmem, smem],
        out_specs=(vmem, vmem),
        scratch_shapes=[
            pltpu.VMEM((rows, 2 * width), F32),
            pltpu.VMEM((2, 2, edge, 2 * width), BF16),
            pltpu.VMEM((2, 2, edge, 2 * width), BF16),
            pltpu.VMEM((np_, rows, width), BF16),
            pltpu.VMEM((np_, rows, width), BF16),
            pltpu.VMEM((2 * width, width), F32),
            pltpu.VMEM((nd, 2 * width // nd, width), F32),
            dma((2, 2)), dma((2, 2)),
            dma((np_,)), dma((np_,)),
            dma((CHUNKS, np_)), dma((CHUNKS, np_)),
            dma((CHUNKS,)), dma((CHUNKS,)),
            dma((nd,)), dma((nd,)),
            dma((nd,)), dma((nd,)),
            dma((nd,)), dma((nd,)),
        ],
        compiler_params=pltpu.CompilerParams(
            collective_id=0, has_side_effects=True, vmem_limit_bytes=40 * 2**20
        ),
        name="filter",
    )(right_side, inverse, coupling, weights)
    return pl.pallas_call(
        functools.partial(solve_kernel, rows * nd),
        out_shape=(
            jax.ShapeDtypeStruct((rows, width), BF16),
            jax.ShapeDtypeStruct((2 * width, 2 * width), F32),
        ),
        in_specs=[vmem, vmem],
        out_specs=(vmem, vmem),
        compiler_params=pltpu.CompilerParams(vmem_limit_bytes=40 * 2**20),
        name="solve",
    )(q, g)


def solution(mesh):
    return jax.shard_map(
        body,
        mesh=mesh,
        in_specs=(
            P(("groups", "dom"), "vec"),
            P("pole", None, ("groups", "dom"), None),
            P(("groups", "dom"), None, None, None),
            P("pole", None),
        ),
        out_specs=(P(("groups", "dom"), "vec"), P("groups", None)),
        check_vma=False,
    )
```

```python
import functools

import jax
import jax.numpy as jnp
from jax import lax
from jax.experimental import pallas as pl
from jax.experimental.pallas import tpu as pltpu
from jax.sharding import PartitionSpec as P

MESH = pl.DeviceIdType.MESH
HI = lax.Precision.HIGHEST
F32 = jnp.float32
BF16 = jnp.bfloat16
CHUNKS = 2


def mm(a, b):
    return jnp.dot(a, b, preferred_element_type=F32)


def tmm(a, b):
    return lax.dot_general(
        a, b, (((0,), (0,)), ((), ())), precision=HI, preferred_element_type=F32
    )


def hmm(a, b):
    return jnp.dot(a, b, precision=HI, preferred_element_type=F32)


def times(a, b):
    return lax.dot_general(
        a, b, (((1,), (1,)), ((), ())), precision=HI, preferred_element_type=F32
    )


def repeat(lo, hi, step):
    if hi - lo <= 16:
        for k in range(lo, hi):
            step(k)
    else:
        lax.fori_loop(lo, hi, lambda k, _: (step(k), 0)[1], 0)


def piece_of(total, owners):
    piece = 8
    while total % piece or total // piece > owners:
        piece += 8
    return piece


def filter_kernel(
    nd, np_, x_hbm, inv_hbm, k_hbm, w_hbm, q_ref, g_ref,
    x_ref, inv_ref, k_ref, w_ref, l_sem, y0, edges, ends, psend, pslot, dsend, dslot,
    cross, gpart, gslot,
    e_send, e_recv, p_send, p_recv, d_send, d_recv, v_send, v_recv,
    q_send, q_recv, h_send, h_recv, r_send, r_recv, a_send, a_recv, f_send, f_recv,
):
    d = lax.axis_index("dom")
    p = lax.axis_index("pole")
    v = lax.axis_index("vec")
    rows, width = x_ref.shape
    edge = k_ref.shape[1]
    last = rows - edge
    share = rows // np_
    tall = share // CHUNKS
    half = width // 2
    owners = nd * np_
    piece = gslot.shape[1]
    pieces = g_ref.shape[1] // piece
    me = d * np_ + p
    a_ref, c_ref = inv_ref.at[0], inv_ref.at[1]
    has_low, has_high = d > 0, d < nd - 1
    other = {"vec": 1 - v}

    def at(k):
        return lax.rem(me + k, owners)

    def device(o):
        return {"dom": lax.div(o, np_), "pole": lax.rem(o, np_)}

    def pole(k):
        return lax.rem(p + k, np_)

    def when_owner(o, act):
        if pieces == owners:
            act()
        else:
            pl.when(o < pieces)(act)

    loads = [pltpu.make_async_copy(x_hbm, x_ref, l_sem.at[0])]
    for n, (lo, count) in enumerate(((0, edge), (last, edge), (edge, last - edge))):
        loads.append(
            pltpu.make_async_copy(
                inv_hbm.at[0, :, lo : lo + count], inv_ref.at[:, lo : lo + count], l_sem.at[n + 1]
            )
        )
    loads.append(pltpu.make_async_copy(k_hbm.at[0], k_ref, l_sem.at[4]))
    loads.append(pltpu.make_async_copy(w_hbm, w_ref, l_sem.at[5]))
    for c in loads:
        c.start()

    barrier = pltpu.get_barrier_semaphore()

    def greet(k):
        pl.semaphore_signal(barrier, inc=1, device_id=device(at(k)), device_id_type=MESH)

    repeat(1, owners, greet)
    pl.semaphore_signal(barrier, inc=1, device_id=other, device_id_type=MESH)

    @pl.when(jnp.logical_not(has_low))
    def _():
        ends[0, 0] = jnp.zeros(ends.shape[2:], BF16)
        ends[1, 0] = jnp.zeros(ends.shape[2:], BF16)

    @pl.when(jnp.logical_not(has_high))
    def _():
        ends[0, 1] = jnp.zeros(ends.shape[2:], BF16)
        ends[1, 1] = jnp.zeros(ends.shape[2:], BF16)

    def copy(src, dst, send, recv, target):
        return pltpu.make_async_remote_copy(
            src_ref=src, dst_ref=dst, send_sem=send, recv_sem=recv,
            device_id=target, device_id_type=MESH,
        )

    def swap_ends(s):
        down = copy(edges.at[s, 0], ends.at[s, 1], e_send.at[s, 1], e_recv.at[s, 1], {"dom": d - 1})
        up = copy(edges.at[s, 1], ends.at[s, 0], e_send.at[s, 0], e_recv.at[s, 0], {"dom": d + 1})
        return down, up

    def start_end(s, n):
        pl.when((has_low, has_high)[n])(swap_ends(s)[n].start)

    def wait_ends(s):
        down, up = swap_ends(s)
        pl.when(has_low)(up.wait_recv)
        pl.when(has_high)(down.wait_recv)
        pl.when(has_high)(up.wait_send)
        pl.when(has_low)(down.wait_send)

    loads[0].wait()
    x = x_ref[...]

    def first(lo):
        y0[lo : lo + edge, :width] = mm(a_ref[lo : lo + edge, :], x)
        y0[lo : lo + edge, width:] = mm(c_ref[lo : lo + edge, :], x)

    for n, lo in enumerate((0, last)):
        loads[n + 1].wait()
        first(lo)
        edges[0, n] = y0[lo : lo + edge, :].astype(BF16)
        if n == 0:
            pl.semaphore_wait(barrier, owners)
        start_end(0, n)

    for c in loads[3:]:
        c.wait()
    for lo in range(edge, last, edge):
        first(lo)
    w0, w1 = w_ref[0, 0], w_ref[0, 1]

    def block(q, i):
        return pl.ds(pl.multiple_of(q * share + i * tall, tall), tall)

    def source_part(at_rows):
        return w0 * y0[at_rows, :width] - w1 * y0[at_rows, width:]

    p_copies = []
    for k in range(1, np_):
        q = pole(k)
        for i in range(CHUNKS):
            psend[k, i * tall : (i + 1) * tall] = source_part(block(q, i)).astype(BF16)
        p_copies.append(copy(psend.at[k], pslot.at[k], p_send.at[k], p_recv.at[k], {"pole": q}))
        p_copies[-1].start()

    wait_ends(0)

    def turned(u):
        return jnp.concatenate([-u[:, width:], u[:, :width]], axis=1)

    tops = [mm(k_ref[n], ends[0, n]) for n in range(2)]
    plain = [t.astype(BF16) for t in tops]
    swapped = [turned(t).astype(BF16) for t in tops]
    for n, lo in enumerate((0, last)):
        total = y0[lo : lo + edge, :]
        for m, col in enumerate((0, last)):
            total += mm(a_ref[lo : lo + edge, col : col + edge], plain[m])
            total += mm(c_ref[lo : lo + edge, col : col + edge], swapped[m])
        edges[1, n] = total.astype(BF16)
        start_end(1, n)
    wait_ends(1)

    tops = [mm(k_ref[n], ends[1, n]) for n in range(2)]
    gs = [(w0 * t[:, :width] - w1 * t[:, width:]).astype(BF16) for t in tops]
    hs = [(-w0 * t[:, width:] - w1 * t[:, :width]).astype(BF16) for t in tops]

    def correction(at_rows):
        total = jnp.zeros((tall, width), F32)
        for m, col in enumerate((0, last)):
            total += mm(a_ref[at_rows, col : col + edge], gs[m])
            total += mm(c_ref[at_rows, col : col + edge], hs[m])
        return total

    d_copies = [[] for _ in range(CHUNKS)]
    for i in range(CHUNKS):
        for k in range(1, np_):
            q = pole(k)
            part = source_part(block(q, i))
            part = part - part.astype(BF16).astype(F32) + correction(block(q, i))
            here = slice(i * tall, (i + 1) * tall)
            dsend[k, here] = part.astype(BF16)
            c = copy(
                dsend.at[k, here], dslot.at[k, here], d_send.at[i, k], d_recv.at[i, k], {"pole": q}
            )
            c.start()
            d_copies[i].append(c)
    for i in range(CHUNKS):
        q_ref[v, block(p, i)] = source_part(block(p, i)) + correction(block(p, i))

    for c in p_copies:
        c.wait()
    v_copies = []
    for i in range(CHUNKS):
        for c in d_copies[i]:
            c.wait()
        total = q_ref[v, block(p, i)]
        here = slice(i * tall, (i + 1) * tall)
        for k in range(1, np_):
            total += pslot[k, here].astype(F32) + dslot[k, here].astype(F32)
        q_ref[v, block(p, i)] = total
        mine = q_ref.at[v, block(p, i)]
        v_copies.append(copy(mine, mine, v_send.at[i], v_recv.at[i], other))
        v_copies[-1].start()

    diagonal = jnp.zeros((width, width), F32)
    below = jnp.zeros((width, width), F32)
    for i in range(CHUNKS):
        mine = q_ref[v, block(p, i)]
        diagonal += tmm(mine, mine)
    gpart[:width] = diagonal
    for i in range(CHUNKS):
        v_copies[i].wait()
        below += tmm(q_ref[1, block(p, i)], q_ref[0, block(p, i)])
    cross[...] = below
    gpart[width:] = cross[pl.ds(pl.multiple_of(v * half, half), half)]

    def part_of(o):
        return pl.ds(pl.multiple_of(o * piece, piece), piece)

    def reduce_copy(k):
        o = at(k)
        return copy(gpart.at[part_of(o)], gslot.at[k], r_send.at[k], r_recv.at[k], device(o))

    repeat(1, owners, lambda k: when_owner(at(k), lambda: reduce_copy(k).start()))

    def whole(q):
        return pl.ds(pl.multiple_of(q * share, share), share)

    q_copies = []
    for k in range(1, np_):
        mine = q_ref.at[v, whole(p)]
        q_copies.append(copy(mine, mine, q_send.at[k], q_recv.at[k], {"pole": pole(k)}))
        q_copies[-1].start()

    def collect():
        repeat(1, owners, lambda k: reduce_copy(k).wait_recv())
        gslot[0] = gpart[part_of(me)]
        total = gslot[0]
        for k in range(1, owners):
            total += gslot[k]
        g_ref[v, part_of(me)] = total

    when_owner(me, collect)

    def gather_copy(k):
        mine = g_ref.at[v, part_of(me)]
        return copy(mine, mine, a_send.at[k], a_recv.at[k], device(at(k)))

    def forward_copy(k):
        theirs = g_ref.at[v, part_of(at(owners - k))]
        return copy(theirs, theirs, f_send.at[k], f_recv.at[k], other)

    when_owner(me, lambda: repeat(1, owners, lambda k: gather_copy(k).start()))
    when_owner(me, lambda: forward_copy(0).start())

    def hand_on(k):
        def act():
            gather_copy(k).wait_recv()
            forward_copy(k).start()

        when_owner(at(owners - k), act)

    repeat(1, owners, hand_on)

    def share_copy(k):
        theirs = q_ref.at[0, whole(pole(np_ - k))]
        return copy(theirs, theirs, h_send.at[k], h_recv.at[k], other)

    for k in range(1, np_):
        q_copies[k - 1].wait_recv()
        pl.when(v == 0)(share_copy(k).start)
    repeat(0, owners, lambda k: when_owner(at(owners - k), forward_copy(k).wait))
    for k in range(1, np_):
        pl.when(v == 1)(share_copy(k).wait_recv)
        pl.when(v == 0)(share_copy(k).wait_send)
        q_copies[k - 1].wait_send()
    repeat(1, owners, lambda k: when_owner(at(k), reduce_copy(k).wait_send))
    when_owner(me, lambda: repeat(1, owners, lambda k: gather_copy(k).wait_send()))


def eliminate(w):
    n = w.shape[0]
    sub = lax.broadcasted_iota(jnp.int32, (8, n), 0)
    lane = lax.broadcasted_iota(jnp.int32, (8, n), 1)
    groups = n // 8
    ws = [w[8 * g : 8 * g + 8] for g in range(groups)]
    es = [(lane == sub + 8 * g).astype(F32) for g in range(groups)]
    upper, lower = [], []
    for b in range(groups):
        k = 8 * b
        pw, pe = ws[b], es[b]
        cols = [jnp.broadcast_to(pw[:, k + j : k + j + 1], (8, n)) for j in range(8)]
        far = [
            [jnp.broadcast_to(ws[g][:, k + j : k + j + 1], (8, n)) for j in range(8)]
            for g in range(b + 1, groups)
        ]
        uw, ue = jnp.zeros_like(pw), jnp.zeros_like(pe)
        for j in range(8):
            at = sub == j
            c = cols[j]
            pivot = c[j : j + 1]
            root = lax.rsqrt(pivot)
            inverse = 1.0 / pivot
            rw, re = pw[j : j + 1], pe[j : j + 1]
            uw = jnp.where(at, rw * root, uw)
            ue = jnp.where(at, re * root, ue)
            rw, re = rw * inverse, re * inverse
            pw = jnp.where(at, rw, pw - c * rw)
            pe = jnp.where(at, re, pe - c * re)
            for m in range(j + 1, 8):
                rc = cols[m][j : j + 1] * inverse
                cols[m] = jnp.where(at, rc, cols[m] - c * rc)
        upper.append(uw)
        lower.append(ue)
        for g in range(b + 1, groups):
            for j in range(8):
                c = far[g - b - 1][j]
                ws[g] = ws[g] - c * pw[j : j + 1]
                es[g] = es[g] - c * pe[j : j + 1]
    u = jnp.concatenate(upper, axis=0)
    l = jnp.concatenate(lower, axis=0)
    row = lax.broadcasted_iota(jnp.int32, (n, n), 0)
    col = lax.broadcasted_iota(jnp.int32, (n, n), 1)
    return jnp.where(row <= col, u, 0.0), jnp.where(row >= col, l, 0.0)


def solve_kernel(rows_total, q_ref, g_ref, basis_ref, factor_ref):
    v = lax.axis_index("vec")
    width = g_ref.shape[2]
    scale = 1.0 / rows_total
    u11, i11 = eliminate(g_ref[0, :width] * scale)
    low = jnp.concatenate([g_ref[0, width:], g_ref[1, width:]], axis=0) * scale
    u12 = times(i11, low)
    schur = g_ref[1, :width] * scale - tmm(u12, u12)
    u22, i22 = eliminate(schur)
    factor_ref[:width, :width] = u11.T
    factor_ref[:width, width:] = jnp.zeros((width, width), F32)
    factor_ref[width:, :width] = u12.T
    factor_ref[width:, width:] = u22.T

    @pl.when(v == 0)
    def _():
        basis_ref[...] = times(q_ref[0], i11).astype(BF16)

    @pl.when(v == 1)
    def _():
        i21 = -hmm(i22, tmm(u12, i11))
        basis_ref[...] = (times(q_ref[0], i21) + times(q_ref[1], i22)).astype(BF16)


def body(right_side, inverse, coupling, weights):
    rows, width = right_side.shape
    edge = coupling.shape[2]
    nd, np_ = lax.axis_size("dom"), lax.axis_size("pole")
    owners = nd * np_
    total = width + width // 2
    vmem = pl.BlockSpec(memory_space=pltpu.VMEM)
    hbm = pl.BlockSpec(memory_space=pltpu.HBM)
    dma = pltpu.SemaphoreType.DMA
    q, g = pl.pallas_call(
        functools.partial(filter_kernel, nd, np_),
        out_shape=(
            jax.ShapeDtypeStruct((2, rows, width), F32),
            jax.ShapeDtypeStruct((2, total, width), F32),
        ),
        in_specs=[hbm, hbm, hbm, hbm],
        out_specs=(vmem, vmem),
        scratch_shapes=[
            pltpu.VMEM((rows, width), BF16),
            pltpu.VMEM((2, rows, rows), BF16),
            pltpu.VMEM((2, edge, edge), BF16),
            pltpu.SMEM((1, 2), F32),
            dma((6,)),
            pltpu.VMEM((rows, 2 * width), F32),
            pltpu.VMEM((2, 2, edge, 2 * width), BF16),
            pltpu.VMEM((2, 2, edge, 2 * width), BF16),
            pltpu.VMEM((np_, rows // np_, width), BF16),
            pltpu.VMEM((np_, rows // np_, width), BF16),
            pltpu.VMEM((np_, rows // np_, width), BF16),
            pltpu.VMEM((np_, rows // np_, width), BF16),
            pltpu.VMEM((width, width), F32),
            pltpu.VMEM((total, width), F32),
            pltpu.VMEM((owners, piece_of(total, owners), width), F32),
            dma((2, 2)), dma((2, 2)),
            dma((np_,)), dma((np_,)),
            dma((CHUNKS, np_)), dma((CHUNKS, np_)),
            dma((CHUNKS,)), dma((CHUNKS,)),
            dma((np_,)), dma((np_,)),
            dma((np_,)), dma((np_,)),
            dma((owners,)), dma((owners,)),
            dma((owners,)), dma((owners,)),
            dma((owners,)), dma((owners,)),
        ],
        compiler_params=pltpu.CompilerParams(
            collective_id=0, has_side_effects=True, vmem_limit_bytes=40 * 2**20
        ),
        name="filter",
    )(right_side, inverse, coupling, weights)
    return pl.pallas_call(
        functools.partial(solve_kernel, rows * nd),
        out_shape=(
            jax.ShapeDtypeStruct((rows, width), BF16),
            jax.ShapeDtypeStruct((2 * width, 2 * width), F32),
        ),
        in_specs=[vmem, vmem],
        out_specs=(vmem, vmem),
        compiler_params=pltpu.CompilerParams(vmem_limit_bytes=40 * 2**20),
        name="solve",
    )(q, g)


def solution(mesh):
    return jax.shard_map(
        body,
        mesh=mesh,
        in_specs=(
            P(("groups", "dom"), "vec"),
            P("pole", None, ("groups", "dom"), None),
            P(("groups", "dom"), None, None, None),
            P("pole", None),
        ),
        out_specs=(P(("groups", "dom"), "vec"), P("groups", None)),
        check_vma=False,
    )
```
